256 devices in a mesh: branch: 64 (over z, y, core), col: 4 (over x).
Axes of the slice: x: 4, y: 4, z: 8, core: 2. Of those that a mesh axis runs over, the one named last changes fastest.
Arguments:
- points_x: bfloat16 [524288, 256], P('branch', 'col'), may hold values from -6 to 6
- near_blocks: bfloat16 [2048, 8, 256, 256], P('branch', None, 'col'), may hold values from -0.125 to 0.125
- near_list: int32 [2048, 8], P('branch'), may hold values from 0 to 2047, as said below
- leaf_basis: bfloat16 [2048, 256, 64], P('branch'), may hold values from -0.375 to 0.375
- leaf_transfer: bfloat16 [2048, 64, 64], P('branch'), may hold values from -0.125 to 0.125
- level_transfer: bfloat16 [3, 64, 64, 64], P(None, 'branch'), may hold values from -0.75 to 0.75
- coupling: bfloat16 [64, 8, 64, 64], P('branch'), may hold values from -0.25 to 0.25
- coupling_list: int32 [64, 8], P('branch'), may hold values from 0 to 63, as said below
Outputs:
- near_field: bfloat16 [524288, 256], P('branch', 'col')
- coupled: float32 [64, 64, 256], P('branch', None, 'col')
- upward: float32 [3, 64, 64, 256], P(None, 'branch', None, 'col')
The draws below stay inside these ranges and needn't reach their ends.
Inputs may be any that keep to these rules, and one draw needn't show every extreme that they name: `near_list`: each entry lies within 2 of its row's leaf index; in every row one entry is the leaf itself and at least two others lie exactly 2 away. `coupling_list`: entry (i, j) is never i, i + 1 or i - 1 modulo 64.
All inputs are finite; a program needn't handle non-finite values.
Results may differ from the reference program's by a relative error of at most 0.0031.
Values may be sent and summed in bfloat16 or wider, within the bound.
No kernel may reach another device: no remote copies, remote signals or barrier semaphores. Data moves between devices by JAX's collectives and lax.ppermute only.
A program may use at most 128 MiB of HBM per device.

```python
import jax
import jax.numpy as jnp
from jax import lax

LEAF = 256
RANK = 64
R = 256
LEAVES_DEV = 32
NEARK = 8
CPLK = 8
UP = 3
HALO_LEAVES = 2
LEAVES = 2048
POINTS = 524288
N_BRANCH = 64


def draw_near_list(key, part):
    key = jax.random.fold_in(key, 11)
    target = jnp.arange(LEAVES, dtype=jnp.int32)[:, None]
    column = jnp.arange(NEARK, dtype=jnp.int32)[None, :]
    offsets = jax.random.randint(key, (LEAVES, NEARK), -HALO_LEAVES, HALO_LEAVES + 1).astype(jnp.int32)
    offsets = jnp.where(column == 0, 0, jnp.where(column == 1, -HALO_LEAVES, jnp.where(column == 2, HALO_LEAVES, offsets)))
    source = target + offsets
    inside = (source >= 0) & (source < LEAVES)
    return jnp.where(inside, source, target - offsets).astype(jnp.int32)


def draw_coupling_list(key, part):
    key = jax.random.fold_in(key, 23)
    owner = jnp.arange(N_BRANCH, dtype=jnp.int32)[:, None]
    column = jnp.arange(CPLK, dtype=jnp.int32)[None, :]
    offsets = jax.random.randint(key, (N_BRANCH, CPLK), 0, N_BRANCH - 3).astype(jnp.int32)
    offsets = jnp.where(column == 0, 0, offsets)
    return ((owner + 2 + offsets) % N_BRANCH).astype(jnp.int32)


def shard_levels(rng, shape, split, least, high):
    def one(axis_at, parts):
        steps = jax.random.uniform(jax.random.fold_in(jax.random.fold_in(rng, 6), axis_at), (parts,), jnp.float32, least / len(split), high / len(split))
        return jnp.repeat(jnp.exp(steps), shape[axis_at] // parts).reshape((-1,) + (1,) * (len(shape) - axis_at - 1))

    factor_of = one(*split[0])
    for cut in split[1:]:
        factor_of = factor_of * one(*cut)
    return factor_of


def centred(own_key, shape, width, bound, split=(), kind=jnp.bfloat16):
    values = width * jax.random.normal(own_key, shape, jnp.float32)
    if split:
        values = values * shard_levels(own_key, shape, split, -0.22, 0.18)
    return jnp.clip(values, -bound, bound).astype(kind)


def setup_inputs(seed: int = 0) -> dict:
    key_list = jax.random.split(jax.random.key(seed), 9)
    return {
        "points_x": centred(key_list[0], (POINTS, R), 1.0, 6.0, ((0, 64), (1, 4))),
        "near_blocks": centred(key_list[1], (LEAVES, NEARK, LEAF, LEAF), (LEAF * NEARK) ** -0.5, 0.125, ((0, 64), (2, 4))),
        "near_list": draw_near_list(jax.random.fold_in(key_list[8], 71), 0),
        "leaf_basis": centred(key_list[3], (LEAVES, LEAF, RANK), LEAF ** -0.5, 0.375, ((0, 64),)),
        "leaf_transfer": centred(key_list[4], (LEAVES, RANK, RANK), (RANK * LEAVES_DEV) ** -0.5, 0.125, ((0, 64),)),
        "level_transfer": centred(key_list[5], (UP, N_BRANCH, RANK, RANK), RANK ** -0.5, 0.75, ((1, 64),)),
        "coupling": centred(key_list[6], (N_BRANCH, CPLK, RANK, RANK), (RANK * CPLK) ** -0.5, 0.25, ((0, 64),)),
        "coupling_list": draw_coupling_list(jax.random.fold_in(key_list[8], 71), 0),
    }


def reference(points_x, near_blocks, near_list, leaf_basis, leaf_transfer, level_transfer, coupling, coupling_list):
    by_leaf = points_x.reshape(LEAVES, LEAF, R)

    def one_leaf(items):
        blocks, ids = items
        sources = by_leaf[ids].astype(jnp.float32)
        return jnp.einsum("krs,ksc->rc", blocks.astype(jnp.float32), sources).astype(jnp.bfloat16)

    near_field = lax.map(one_leaf, (near_blocks, near_list)).reshape(POINTS, R)
    projected = jnp.einsum("lsa,lsc->lac", leaf_basis.astype(jnp.float32), by_leaf.astype(jnp.float32)).astype(jnp.bfloat16)
    per_leaf = jnp.einsum("lab,lac->lbc", leaf_transfer.astype(jnp.float32), projected.astype(jnp.float32))
    node = per_leaf.reshape(N_BRANCH, LEAVES_DEV, RANK, R).sum(axis=1)
    terms = jnp.einsum("kiab,iac->kibc", level_transfer.astype(jnp.float32), node, precision=lax.Precision.HIGHEST)
    levels = []
    for level in range(UP):
        span = 2 ** (level + 1)
        grouped = terms[level].reshape(N_BRANCH // span, span, RANK, R).sum(axis=1)
        levels.append(jnp.repeat(grouped, span, axis=0))
    upward = jnp.stack(levels)
    coupled = jnp.einsum("ijab,ijbc->iac", coupling.astype(jnp.float32), node[coupling_list], precision=lax.Precision.HIGHEST)
    return near_field, coupled, upward
```

```python
import functools

import jax
import jax.numpy as jnp
from jax import lax
from jax.experimental import pallas as pl
from jax.experimental.pallas import tpu as pltpu
from jax.sharding import PartitionSpec as P

HALO_LEAVES = 2
PARTS = 4
VMEM_LIMIT = 16 << 20
NT = (((1,), (1,)), ((), ()))
F32 = jnp.float32
BF16 = jnp.bfloat16


def shifted(value, axis, step):
    size = lax.axis_size(axis)
    return lax.ppermute(value, axis, [(i, (i + step) % size) for i in range(size)])


def along_branch(value, step):
    size = lax.axis_size("branch")
    pairs = [(i, i + step) for i in range(size) if 0 <= i + step < size]
    return lax.ppermute(value, "branch", pairs)


def near_kernel(pieces, count, out_rows, steps, ids_ref, blocks_ref, *refs):
    ins, outs = refs[:count], refs[count : count + len(out_rows)]
    held, sems = refs[count + len(out_rows) :]
    step = pl.program_id(0)
    leaves, blocks, rows, leaf = blocks_ref.shape

    @pl.when(step == 0)
    def load():
        copies = []
        for n, (source, row, rows_of, at, lane, wide) in enumerate(pieces):
            taken = ins[source].at[row : row + rows_of, lane : lane + wide]
            place = held.at[at[0] : at[0] + rows_of, at[1] : at[1] + wide]
            copies.append(pltpu.make_async_copy(taken, place, sems.at[n]))
        for copy in copies:
            copy.start()
        for copy in copies:
            copy.wait()

    first = lax.axis_index("branch") * (leaves * steps) - HALO_LEAVES
    for pair in range(0, leaves, 2):
        sums = []
        for l in (pair, pair + 1):
            total = None
            for k in range(blocks):
                source = ids_ref[k, step * leaves + l] - first
                lanes = pl.ds(pl.multiple_of(source * leaf, leaf), leaf)
                part = lax.dot_general(
                    held[:, lanes], blocks_ref[l, k], NT, preferred_element_type=F32
                )
                total = part if total is None else total + part
            sums.append(total)
        both = jnp.concatenate(sums, axis=1).astype(BF16)
        row = 0
        for high, out in zip(out_rows, outs):
            out[:, pair * rows : (pair + 2) * rows] = both[row : row + high]
            row += high


def near_rows(ids, near_blocks, pieces, arrays, out_rows, name):
    all_leaves, blocks, rows, leaf = near_blocks.shape
    leaves = 8
    steps = all_leaves // leaves
    columns = sum(out_rows)
    return pl.pallas_call(
        functools.partial(near_kernel, pieces, len(arrays), out_rows, steps),
        grid_spec=pltpu.PrefetchScalarGridSpec(
            num_scalar_prefetch=1,
            grid=(steps,),
            in_specs=[pl.BlockSpec((leaves, blocks, rows, leaf), lambda i, _: (i, 0, 0, 0))]
            + [pl.BlockSpec(memory_space=pl.ANY)] * len(arrays),
            out_specs=[pl.BlockSpec((high, leaves * rows), lambda i, _: (0, i)) for high in out_rows],
            scratch_shapes=[
                pltpu.VMEM((columns, (all_leaves + 2 * HALO_LEAVES) * leaf), BF16),
                pltpu.SemaphoreType.DMA((len(pieces),)),
            ],
        ),
        out_shape=[jax.ShapeDtypeStruct((high, all_leaves * rows), BF16) for high in out_rows],
        compiler_params=pltpu.CompilerParams(vmem_limit_bytes=VMEM_LIMIT),
        cost_estimate=pl.CostEstimate(
            flops=2 * columns * all_leaves * blocks * rows * leaf,
            bytes_accessed=near_blocks.size * 2,
            transcendentals=0,
        ),
        name=name,
    )(ids, near_blocks, *arrays)


def assemble_kernel(places, *refs):
    ins, out = refs[:-3], refs[-3]
    held, sems = refs[-2:]
    step = pl.program_id(0)
    me = lax.axis_index("col")
    rows = 64
    wide = out.shape[1] // PARTS

    @pl.when(step == 0)
    def load():
        copies = []
        for n, (ahead, row) in enumerate(places):
            part = lax.rem(me + ahead, PARTS)
            place = held.at[part, row : row + ins[n].shape[0], :]
            copies.append(pltpu.make_async_copy(ins[n], place, sems.at[n]))
        for copy in copies:
            copy.start()
        for copy in copies:
            copy.wait()

    for pair in range(wide // (2 * rows)):
        lanes = pl.ds(pl.multiple_of(step * wide + pair * 2 * rows, 2 * rows), 2 * rows)
        parts = [held[p, :, lanes] for p in range(PARTS)]
        for l in range(2):
            at = (2 * pair + l) * PARTS * rows
            halves = [part[:, l * rows : (l + 1) * rows] for part in parts]
            out[:, at : at + 2 * rows] = jnp.concatenate(halves[:2], axis=1)
            out[:, at + 2 * rows : at + 4 * rows] = jnp.concatenate(halves[2:], axis=1)


def assemble(places, arrays, columns, points):
    steps = 4
    return pl.pallas_call(
        functools.partial(assemble_kernel, places),
        grid=(steps,),
        in_specs=[pl.BlockSpec(memory_space=pl.ANY)] * len(arrays),
        out_specs=pl.BlockSpec((columns, points // steps), lambda i: (0, i)),
        scratch_shapes=[
            pltpu.VMEM((PARTS, columns, points // PARTS), BF16),
            pltpu.SemaphoreType.DMA((len(places),)),
        ],
        out_shape=jax.ShapeDtypeStruct((columns, points), BF16),
        compiler_params=pltpu.CompilerParams(vmem_limit_bytes=VMEM_LIMIT),
        name="assemble",
    )(*arrays)


def coupled_kernel(list_ref, coupling_ref, everyone, out, held, sems):
    count, rank = coupling_ref.shape[:2]
    copies = [
        pltpu.make_async_copy(everyone.at[list_ref[0, j]], held.at[j], sems.at[j]) for j in range(count)
    ]
    for copy in copies:
        copy.start()
    for copy in copies:
        copy.wait()
    total = jnp.zeros(out.shape, F32)
    for j in range(count):
        packed = held[j]
        node = jnp.concatenate([packed[:, :rank], packed[:, rank:]], axis=0)
        total += jnp.dot(
            coupling_ref[j].astype(F32), node, precision=lax.Precision.HIGHEST, preferred_element_type=F32
        )
    out[...] = total


def coupled_rows(coupling_list, coupling, everyone):
    count, rank = coupling.shape[:2]
    return pl.pallas_call(
        coupled_kernel,
        in_specs=[
            pl.BlockSpec(memory_space=pltpu.SMEM),
            pl.BlockSpec(memory_space=pltpu.VMEM),
            pl.BlockSpec(memory_space=pl.ANY),
        ],
        out_specs=pl.BlockSpec(memory_space=pltpu.VMEM),
        scratch_shapes=[
            pltpu.VMEM((count,) + everyone.shape[1:], F32),
            pltpu.SemaphoreType.DMA((count,)),
        ],
        out_shape=jax.ShapeDtypeStruct((rank, rank), F32),
        name="coupled",
    )(coupling_list, coupling, everyone)


def body(
    points_x,
    near_blocks,
    near_list,
    leaf_basis,
    leaf_transfer,
    level_transfer,
    coupling,
    coupling_list,
):
    leaves_here = near_blocks.shape[0]
    leaf = leaf_basis.shape[1]
    points, width = points_x.shape
    edge = HALO_LEAVES * leaf
    half = width // 2
    columns = points_x.T
    ids = near_list.T
    low, high = columns[:half], columns[half:]

    left_low = shifted(low, "col", 1)
    right_high = shifted(high, "col", -1)
    before = along_branch(columns[:, points - edge :], 1)
    after = along_branch(columns[:, :edge], -1)
    edges = jnp.concatenate([before, after], axis=1)
    left_rest = shifted(jnp.concatenate([high, edges[half:], edges[:half]], axis=1), "col", 1)
    right_rest = shifted(jnp.concatenate([low, edges[:half], edges[half:]], axis=1), "col", -1)
    far_edges = shifted(edges, "col", 2)
    far_low = shifted(left_low, "col", 1)
    far_high = shifted(right_high, "col", -1)

    local_x = points_x.reshape(leaves_here, leaf, width)
    projected = jnp.einsum("lsa,lsc->lac", leaf_basis, local_x, preferred_element_type=F32).astype(BF16)
    node = jnp.einsum("lab,lac->bc", leaf_transfer, projected, preferred_element_type=F32)
    rank = node.shape[0]
    packed = jnp.concatenate([node[: rank // 2], node[rank // 2 :]], axis=1)
    copies = jnp.broadcast_to(packed[None], (lax.axis_size("branch"),) + packed.shape)
    everyone = lax.all_to_all(copies, "branch", split_axis=0, concat_axis=0, tiled=True)
    terms = jnp.einsum(
        "kab,ac->kbc",
        level_transfer[:, 0].astype(F32),
        node,
        precision=lax.Precision.HIGHEST,
    )
    levels = []
    summed = terms
    for bit in range(terms.shape[0]):
        pairs = [(i, i ^ 2**bit) for i in range(lax.axis_size("branch"))]
        summed = summed + lax.ppermute(summed, "branch", pairs)
        levels.append(summed[0])
        summed = summed[1:]
    upward = jnp.stack(levels)[:, None]

    end = edge + points
    (own,) = near_rows(
        ids,
        near_blocks,
        [(0, 0, width, (0, 0), 0, edge), (0, 0, width, (0, end), edge, edge), (1, 0, width, (0, edge), 0, points)],
        [edges, columns, left_low, right_high],
        [width],
        "near_own",
    )
    pieces = []
    for n, top in ((0, 0), (2, width)):
        swap = half if n else 0
        main, other = top + swap, top + half - swap
        pieces += [
            (n, 0, half, (main, edge), 0, points),
            (n + 1, 0, half, (main, 0), points + 2 * edge, edge),
            (n + 1, 0, half, (main, end), points + 3 * edge, edge),
            (n + 1, 0, half, (other, edge), 0, points),
            (n + 1, 0, half, (other, 0), points, edge),
            (n + 1, 0, half, (other, end), points + edge, edge),
        ]
    to_left, to_right = near_rows(
        ids, near_blocks, pieces, [left_low, left_rest, right_high, right_rest], [width] * 2, "near_sides"
    )
    (to_far,) = near_rows(
        ids,
        near_blocks,
        [
            (0, 0, width, (0, 0), 0, edge),
            (0, 0, width, (0, end), edge, edge),
            (1, 0, half, (0, edge), 0, points),
            (2, 0, half, (half, edge), 0, points),
        ],
        [far_edges, far_low, far_high],
        [width],
        "near_far",
    )
    from_right = shifted(to_left, "col", -1)
    from_left = shifted(to_right, "col", 1)
    from_far = shifted(to_far, "col", 2)
    coupled = coupled_rows(coupling_list, coupling[0], everyone)
    near_field = assemble(
        [(0, 0), (1, 0), (3, 0), (2, 0)], [own, from_right, from_left, from_far, coupled, upward], width, points
    )
    return (near_field.T, coupled[None], upward)


def solution(mesh):
    placed = (
        P("branch", "col"),
        P("branch", None, "col", None),
        P("branch", None),
        P("branch", None, None),
        P("branch", None, None),
        P(None, "branch", None, None),
        P("branch", None, None, None),
        P("branch", None),
    )
    return jax.shard_map(
        body,
        mesh=mesh,
        in_specs=placed,
        out_specs=(P("branch", "col"), P("branch", None, "col"), P(None, "branch", None, "col")),
        check_vma=False,
    )
```
